32 devices in a mesh: policy: 4 (over y, x), zero: 8 (over z, core).
Axes of the slice: x: 2, y: 2, z: 4, core: 2. Of those that a mesh axis runs over, the one named last changes fastest.
Arguments:
- acts: bfloat16 [4, 5120, 4608], P('policy', 'zero'), may hold values from -6 to 6
- cotan: bfloat16 [4, 5120, 1024], P('policy', 'zero'), may hold values from -6 to 6
- advantage: int32 [4, 40], P('policy', 'zero'), may hold values from -4 to 4
- merge_ratio: int32 [4], replicated, may hold values from 1 to 8
- weight: bfloat16 [4, 4608, 1024], P('policy', 'zero'), may hold values from -0.3125 to 0.3125
- anchor: float32 [4, 4608, 1024], P('policy', 'zero'), may hold values from -0.3125 to 0.3125
- init: bfloat16 [4608, 1024], P('zero'), may hold values from -0.62 to 0.62
Outputs:
- anchor_new: float32 [4, 4608, 1024], P('policy', 'zero')
- merged: bfloat16 [4608, 1024], P('zero')
- merged_out: float32 [4, 5120, 1024], P('policy', 'zero')
The draws below stay inside these ranges and needn't reach their ends.
All inputs are finite; a program needn't handle non-finite values.
Results may differ from the reference program's by a relative error of at most 0.015.
Values may be sent and summed in bfloat16 or wider, within the bound.
A program may use at most 128 MiB of HBM per device.

```python
import math
import jax
import jax.numpy as jnp
from jax import lax

D = 4608
KV = 1024
SEQ = 128
TOK_DEV = 640
POLICIES = 4
TOKENS = 5120
N_ZERO = 8


def draw_init(key, part):
    key = jax.random.fold_in(key, 7)
    first, second = jax.random.split(key)
    rows = jnp.arange(D, dtype=jnp.float32)[:, None]
    base = jnp.clip(jax.random.normal(first, (D, KV), jnp.float32), -5.0, 5.0)
    spread = jnp.exp(jax.random.uniform(second, (D, 1), jnp.float32, 0.0, math.log(4.0)))
    return (0.01 * base * spread * jnp.exp(rows / D * math.log(3.0))).astype(jnp.bfloat16)


def touch_ends(array, own_key, least, high):
    dims = array.shape
    index_at = [jax.random.randint(jax.random.fold_in(own_key, axis), (), 0, dims[axis]) for axis in range(len(dims))]
    array = array.at[tuple(index_at)].set(least)
    longest = dims.index(max(dims))
    index_at[longest] = (index_at[longest] + 1) % dims[longest]
    return array.at[tuple(index_at)].set(high)


def block_levels(key, extent, cuts, low, largest):
    loudness, own = 1.0, jax.random.fold_in(key, 6)
    for position, blocks in cuts:
        heights = jnp.exp(jax.random.uniform(jax.random.fold_in(own, position), (blocks,), jnp.float32, low / len(cuts), largest / len(cuts)))
        loudness = loudness * jnp.repeat(heights, extent[position] // blocks).reshape([-1 if axis == position else 1 for axis in range(len(extent))])
    return loudness


def noise(own_key, extent, scale, most, pieces=(), kind=jnp.bfloat16):
    gain = block_levels(own_key, extent, pieces, -0.22, 0.18) if pieces else 1.0
    array = jax.random.normal(own_key, extent, jnp.float32) * scale * gain
    return jnp.minimum(jnp.maximum(array, -most), most).astype(kind)


def setup_inputs(seed: int = 0) -> dict:
    seeds = jax.random.split(jax.random.key(seed), 8)
    acts = noise(seeds[0], (POLICIES, TOKENS, D), 1.0, 6.0, ((0, 4), (1, 8)))
    cotan = noise(seeds[1], (POLICIES, TOKENS, KV), 1.0, 6.0, ((0, 4), (1, 8)))
    advantage = touch_ends(jax.random.randint(seeds[2], (POLICIES, TOKENS // SEQ), -4, 5), jax.random.fold_in(seeds[2], 1), -4, 4).astype(jnp.int32)
    merge_ratio = touch_ends(jax.random.randint(seeds[3], (POLICIES,), 1, 9), jax.random.fold_in(seeds[3], 1), 1, 8).astype(jnp.int32)
    weight = noise(seeds[4], (POLICIES, D, KV), 0.02, 0.3125, ((0, 4), (1, 8)))
    anchor = noise(seeds[5], (POLICIES, D, KV), 0.02, 0.3125, ((0, 4), (1, 8)), jnp.float32)
    init = draw_init(jax.random.fold_in(seeds[7], 71), 0)
    return {"acts": acts, "cotan": cotan, "advantage": advantage, "merge_ratio": merge_ratio, "weight": weight, "anchor": anchor, "init": init}


step_size = 0.02
ema_decay = 0.9

def reference(acts, cotan, advantage, merge_ratio, weight, anchor, init):
    tokens = acts.shape[1]
    ratio = merge_ratio.astype(jnp.float32)
    share = ratio / jnp.sum(ratio)
    init_wide = init.astype(jnp.float32)
    anchors = []
    target = jnp.float32(0.0)
    mixed = jnp.zeros(init.shape, jnp.float32)
    for policy_idx in range(POLICIES):
        levels = jnp.repeat(advantage[policy_idx].astype(jnp.float32) * 0.25, SEQ)
        scaled = (cotan[policy_idx].astype(jnp.float32) * levels[:, None]).astype(jnp.bfloat16)
        act_blocks = acts[policy_idx].reshape(N_ZERO, TOK_DEV, D)
        scaled_blocks = scaled.reshape(N_ZERO, TOK_DEV, KV)

        def add_block(total, pair):
            block_acts, block_scaled = pair
            term = lax.dot_general(block_acts, block_scaled, (((0,), (0,)), ((), ())), preferred_element_type=jnp.float32)
            return (total + term.astype(jnp.bfloat16).astype(jnp.float32), None)
        grad, unused = lax.scan(add_block, jnp.zeros((D, KV), jnp.float32), (act_blocks, scaled_blocks))
        updated = weight[policy_idx].astype(jnp.float32) - step_size * grad / math.sqrt(tokens)
        anchors.append(ema_decay * anchor[policy_idx] + (1.0 - ema_decay) * updated)
        task = updated - init_wide
        target = target + share[policy_idx] * jnp.sqrt(jnp.sum(task * task))
        mixed = mixed + share[policy_idx] * task
    mixed_sq = jnp.sum(mixed * mixed)
    merged = (init_wide + mixed * (target / jnp.sqrt(mixed_sq))).astype(jnp.bfloat16)
    outputs = []
    for policy_idx in range(POLICIES):
        outputs.append(jnp.dot(acts[policy_idx], merged, preferred_element_type=jnp.float32))
    return (jnp.stack(anchors), merged, jnp.stack(outputs))
```

```python
import functools
import math

import jax
import jax.numpy as jnp
from jax import lax
from jax.experimental import pallas as pl
from jax.experimental.pallas import tpu as pltpu
from jax.sharding import PartitionSpec as P

SEQ = 128
STEP = 0.02
DECAY = 0.9
CHUNKS = 3
SUB = 16
F32 = jnp.float32
BF16 = jnp.bfloat16
MESH = pl.DeviceIdType.MESH


def flip(index, mask):
    out, bit = 0, 1
    while bit <= mask:
        digit = (index // bit) % 2
        out = out + bit * ((1 - digit) if mask & bit else digit)
        bit *= 2
    return out + (index // bit) * bit


def remote(src, dst, send, recv, **where):
    return pltpu.make_async_remote_copy(
        src_ref=src, dst_ref=dst, send_sem=send, recv_sem=recv, device_id=where, device_id_type=MESH
    )


def kernel(
    n_pol, n_zero, total_tokens,
    acts, cotan, adv, ratio, weight, anchor, init,
    anchor_out, merged_out, result,
    scaled, part, sib, up, dn, grad, ubuf, prec, mixed, mg, nsq, msq, ztile, ptile,
    sib_s, sib_r, up_s, up_r, dn_s, dn_r, pol_s, pol_r, zs_s, zs_r, ps_s, ps_r, ag_r, line_s, peer_s, core_s, relay_s,
):
    p = lax.axis_index("policy")
    b = lax.axis_index("zero")
    z, c = b // 2, b % 2
    nz = n_zero // 2
    rows, width = init.shape
    depth = acts.shape[1]
    pair = 2 * rows
    cw = width // n_pol
    R = rows // CHUNKS
    other = b + 1 - 2 * c
    sends = []

    def post(cond, make):
        @pl.when(cond)
        def _():
            make().start()
        sends.append((cond, make))

    barrier = pltpu.get_barrier_semaphore()
    for j in range(1, n_zero):
        pl.semaphore_signal(barrier, inc=1, device_id={"zero": lax.rem(b + j, n_zero)}, device_id_type=MESH)
    for j in range(1, n_pol):
        pl.semaphore_signal(barrier, inc=1, device_id={"policy": flip(p, j)}, device_id_type=MESH)

    for s in range(adv.shape[1]):
        level = adv[0, s].astype(F32) * 0.25

        @pl.loop(0, SEQ // SUB)
        def _(i):
            at = pl.ds(pl.multiple_of(s * SEQ + i * SUB, SUB), SUB)
            scaled[at, :] = (cotan[at, :].astype(F32) * level).astype(BF16)

    nsq[...] = jnp.zeros_like(nsq)
    msq[...] = jnp.zeros_like(msq)
    pl.semaphore_wait(barrier, n_zero - 1 + n_pol - 1)

    T = 384

    def tiles(first, count):
        @pl.loop(0, count)
        def _(j):
            at = pl.ds(pl.multiple_of(first + j * T, 128), T)
            part[at, :] = lax.dot_general(
                acts[:, at], scaled[...], (((0,), (0,)), ((), ())), preferred_element_type=F32
            ).astype(BF16)

    def to_sibling(d):
        def make():
            src = part.at[pl.ds(pl.multiple_of(d * pair + (1 - c) * rows, 16), rows), :]
            return remote(src, sib.at[d], sib_s.at[d], sib_r.at[d], zero=other)
        make().start()
        sends.append((None, make))

    order = []
    for i in range((nz + 1) // 2):
        order += [nz - 1 - i] + ([i] if i != nz - 1 - i else [])
    if pair % T == 0:
        for d in order:
            tiles(d * pair, pair // T)
            to_sibling(d)
    else:
        tiles(0, depth // T)
        for d in order:
            to_sibling(d)

    def sib_wait(d):
        remote(sib.at[d], sib.at[d], sib_s.at[d], sib_r.at[d], zero=other).wait_recv()

    def relay(k):
        for i in range(nz - 1):
            for (d, here, end, first_, recv, r_sem, s_sem, slot, step) in (
                (nz - 1 - i, z < nz - 1 - i, z == 0, 0, up, up_r, up_s, nz - 2 - i, 2),
                (i, z > i, z == nz - 1, nz - 1, dn, dn_r, dn_s, i, -2),
            ):
                mine = pl.ds(k * R, R)

                def make(d=d, recv=recv, r_sem=r_sem, s_sem=s_sem, slot=slot, step=step, k=k, i=i, mine=mine):
                    src = part.at[pl.ds(pl.multiple_of(d * pair + c * rows + k * R, 16), R), :]
                    return remote(
                        src, recv.at[slot, mine, :], s_sem.at[slot, k], r_sem.at[slot, k], zero=b + step
                    )

                def add(with_recv, d=d, recv=recv, slot=slot):
                    @pl.loop(0, R // SUB)
                    def _(t):
                        own = pl.ds(pl.multiple_of(d * pair + c * rows + k * R + t * SUB, SUB), SUB)
                        at = pl.ds(pl.multiple_of(k * R + t * SUB, SUB), SUB)
                        acc = part[own, :].astype(F32) + sib[d, at, :].astype(F32)
                        if with_recv:
                            acc = acc + recv[slot, at, :].astype(F32)
                        part[own, :] = acc.astype(BF16)

                if k == 0:
                    @pl.when(here)
                    def _():
                        sib_wait(d)

                @pl.when(jnp.logical_and(here, end))
                def _():
                    add(False)

                @pl.when(jnp.logical_and(here, jnp.logical_not(end)))
                def _():
                    remote(
                        recv.at[slot, mine, :], recv.at[slot, mine, :], s_sem.at[slot, k], r_sem.at[slot, k], zero=b
                    ).wait_recv()
                    add(True)

                post(here, make)

    share = jnp.full((8, 128), ratio[p].astype(F32), F32)
    whole = 0
    for q in range(n_pol):
        whole = whole + ratio[q]
    whole = jnp.full((8, 128), whole.astype(F32), F32)
    share = (share / whole)[0:1, 0:1]
    factor = STEP / math.sqrt(total_tokens)

    def final(k):
        mine = pl.ds(k * R, R)
        if k == 0:
            sib_wait(z)

        @pl.when(z > 0)
        def _():
            slot = z - 1
            remote(up.at[slot, mine, :], up.at[slot, mine, :], up_s.at[slot, k], up_r.at[slot, k], zero=b).wait_recv()

        @pl.when(z < nz - 1)
        def _():
            remote(dn.at[z, mine, :], dn.at[z, mine, :], dn_s.at[z, k], dn_r.at[z, k], zero=b).wait_recv()

        @pl.loop(0, R // SUB)
        def _(t):
            at = pl.ds(pl.multiple_of(k * R + t * SUB, SUB), SUB)
            own = pl.ds(pl.multiple_of(b * rows + k * R + t * SUB, SUB), SUB)
            grad[...] = part[own, :].astype(F32) + sib[z, at, :].astype(F32)

            @pl.when(z > 0)
            def _():
                grad[...] += up[z - 1, at, :].astype(F32)

            @pl.when(z < nz - 1)
            def _():
                grad[...] += dn[z, at, :].astype(F32)

            updated = weight[at, :].astype(F32) - factor * grad[...]
            anchor_out[at, :] = DECAY * anchor[at, :] + (1.0 - DECAY) * updated
            task = updated - init[at, :].astype(F32)
            sq = task * task
            nsq[...] += sq[:8] + sq[8:]
            term = (share * updated).astype(BF16)
            for q in range(n_pol):
                ubuf[q, at, :] = term[:, q * cw:(q + 1) * cw]

        for j in range(1, n_pol):
            def make(j=j):
                q = flip(p, j)
                return remote(
                    ubuf.at[q, mine, :], prec.at[j - 1, mine, :], pol_s.at[j - 1, k], pol_r.at[j - 1, k], policy=q
                )
            make().start()
            sends.append((None, make))

    columns = pl.ds(pl.multiple_of(p * cw, 128), cw)

    def mix(k):
        mine = pl.ds(k * R, R)
        for j in range(1, n_pol):
            ref = prec.at[j - 1, mine, :]
            remote(ref, ref, pol_s.at[j - 1, k], pol_r.at[j - 1, k], policy=p).wait_recv()

        @pl.loop(0, R // SUB)
        def _(t):
            at = pl.ds(pl.multiple_of(k * R + t * SUB, SUB), SUB)
            acc = ubuf[p, at, :].astype(F32)
            for j in range(1, n_pol):
                acc = acc + prec[j - 1, at, :].astype(F32)
            acc = acc - init[at, columns].astype(F32)
            mixed[at, :] = acc
            sq = acc * acc
            msq[...] += sq[:8] + sq[8:]

    for k in range(CHUNKS):
        relay(k)
        if k >= 1:
            final(k - 1)
        if k >= 2:
            mix(k - 2)
    final(CHUNKS - 1)
    for k in range(max(CHUNKS - 2, 0), CHUNKS):
        mix(k)

    ztile[b, 0] = jnp.full((8, 128), jnp.sum(nsq[...]), F32)
    ztile[b, 1] = jnp.full((8, 128), jnp.sum(msq[...]), F32)
    for j in range(1, n_zero):
        def make(j=j):
            return remote(ztile.at[b], ztile.at[b], zs_s.at[j], zs_r.at[j], zero=lax.rem(b + j, n_zero))
        make().start()
        sends.append((None, make))
    result[...] = jnp.zeros_like(result)
    for j in range(1, n_zero):
        ref = ztile.at[lax.rem(b + n_zero - j, n_zero)]
        remote(ref, ref, zs_s.at[j], zs_r.at[j], zero=b).wait_recv()
    ptile[p, 0] = jnp.sum(ztile[:, 0], axis=0)
    ptile[p, 1] = jnp.sum(ztile[:, 1], axis=0)
    for j in range(1, n_pol):
        def make(j=j):
            return remote(ptile.at[p], ptile.at[p], ps_s.at[j], ps_r.at[j], policy=flip(p, j))
        make().start()
        sends.append((None, make))
    for j in range(1, n_pol):
        ref = ptile.at[flip(p, j)]
        remote(ref, ref, ps_s.at[j], ps_r.at[j], policy=p).wait_recv()
    target = jnp.zeros((8, 128), F32)
    mixed_sq = jnp.zeros((8, 128), F32)
    for q in range(n_pol):
        target = target + jnp.full((8, 128), ratio[q].astype(F32), F32) / whole * jnp.sqrt(ptile[q, 0])
        mixed_sq = mixed_sq + ptile[q, 1]
    scale = (target / jnp.sqrt(mixed_sq))[0:1, 0:1]

    @pl.loop(0, rows // SUB)
    def _(t):
        at = pl.ds(pl.multiple_of(t * SUB, SUB), SUB)
        own = pl.ds(pl.multiple_of(b * rows + t * SUB, SUB), SUB)
        mg[p, own, :] = (init[at, columns].astype(F32) + mixed[at, :] * scale).astype(BF16)

    square = n_pol == 4
    direct = (1, 2) if square else tuple(range(1, n_pol))
    half = rows // 2

    def piece(q, block):
        return mg.at[q, pl.ds(pl.multiple_of(block * rows, 16), rows), :]

    def halves(q, block, h):
        return mg.at[q, pl.ds(pl.multiple_of(block * rows + h * half, 16), half), :]

    def arrived(ref, sem):
        remote(ref, ref, sem, sem, zero=b).wait_recv()

    def offsets(t):
        if t < 0 or t >= nz:
            return []
        return [0] if t == 0 else [-t, t]

    def valid(o):
        return jnp.logical_and(z + o >= 0, z + o < nz)

    def stage_line(t):
        for o in offsets(t):
            ok = valid(o)
            zz = z + o
            bb = 2 * zz + c
            if t:
                @pl.when(ok)
                def _():
                    arrived(piece(p, bb), ag_r.at[0, bb])
            if o <= 0:
                post(jnp.logical_and(ok, z < nz - 1), lambda zz=zz, bb=bb: remote(
                    piece(p, bb), piece(p, bb), line_s.at[0, zz], ag_r.at[0, bb], zero=b + 2))
            if o >= 0:
                post(jnp.logical_and(ok, z > 0), lambda zz=zz, bb=bb: remote(
                    piece(p, bb), piece(p, bb), line_s.at[1, zz], ag_r.at[0, bb], zero=b - 2))
            for j in direct:
                post(ok, lambda zz=zz, bb=bb, j=j: remote(
                    piece(p, bb), piece(p, bb), peer_s.at[j, zz], ag_r.at[j, bb], policy=flip(p, j)))
            post(ok, lambda zz=zz, bb=bb: remote(
                piece(p, bb), piece(p, bb), core_s.at[0, zz], ag_r.at[0, bb], zero=other))

    def stage_peer(t):
        for o in offsets(t):
            ok = valid(o)
            zz = z + o
            bb = 2 * zz + c
            for j in direct:
                q = flip(p, j)

                @pl.when(ok)
                def _(j=j, q=q):
                    arrived(piece(q, bb), ag_r.at[j, bb])
                if square:
                    post(ok, lambda zz=zz, bb=bb, j=j, q=q: remote(
                        halves(q, bb, j - 1), halves(q, bb, j - 1), relay_s.at[j - 1, zz], ag_r.at[2 + j, bb],
                        policy=flip(p, 3 - j)))
                post(ok, lambda zz=zz, bb=bb, j=j, q=q: remote(
                    piece(q, bb), piece(q, bb), core_s.at[j, zz], ag_r.at[j, bb], zero=other))

    def stage_diagonal(t):
        if not square:
            return
        for o in offsets(t):
            ok = valid(o)
            zz = z + o
            bb = 2 * zz + c
            q = flip(p, 3)
            for h in (0, 1):
                @pl.when(ok)
                def _(h=h):
                    arrived(halves(q, bb, h), ag_r.at[3 + h, bb])
                post(ok, lambda zz=zz, bb=bb, h=h, q=q: remote(
                    halves(q, bb, h), halves(q, bb, h), core_s.at[3 + h, zz], ag_r.at[3 + h, bb], zero=other))

    def multiply(first, count):
        k_at = pl.ds(pl.multiple_of(first, 128), count)

        @pl.loop(0, n_pol)
        def _(q):
            n_at = pl.ds(pl.multiple_of(q * cw, 128), cw)
            result[:, n_at] += jnp.dot(acts[:, k_at], mg[q, k_at, :], preferred_element_type=F32)

    def stage_multiply(t):
        for o in offsets(t):
            zz = z + o
            bs = 2 * zz + 1 - c

            @pl.when(valid(o))
            def _():
                arrived(piece(p, bs), ag_r.at[0, bs])
                for j in direct:
                    arrived(piece(flip(p, j), bs), ag_r.at[j, bs])
                if square:
                    for h in (0, 1):
                        arrived(halves(flip(p, 3), bs, h), ag_r.at[3 + h, bs])
                if pair % 128 == 0:
                    multiply(zz * pair, pair)

    for t in range(nz + 3):
        stage_line(t)
        stage_peer(t - 1)
        stage_diagonal(t - 2)
        stage_multiply(t - 3)
    if pair % 128 != 0:
        tile = math.lcm(pair, 128)

        @pl.loop(0, depth // tile)
        def _(i):
            multiply(i * tile, tile)

    for q in range(n_pol):
        merged_out[:, q * cw:(q + 1) * cw] = mg[q, pl.ds(pl.multiple_of(b * rows, 16), rows), :]

    for cond, make in sends:
        if cond is None:
            make().wait_send()
        else:
            @pl.when(cond)
            def _(make=make):
                make().wait_send()


def on_device(n_pol, n_zero, acts, cotan, advantage, merge_ratio, weight, anchor, init):
    tokens, depth = acts.shape[1:]
    rows, width = init.shape
    nz, cw = n_zero // 2, width // n_pol
    dma = pltpu.SemaphoreType.DMA
    vmem = pl.BlockSpec(memory_space=pltpu.VMEM)
    smem = pl.BlockSpec(memory_space=pltpu.SMEM)
    lanes = max(n_pol, 5)
    anchor_new, merged, result = pl.pallas_call(
        functools.partial(kernel, n_pol, n_zero, tokens * n_zero),
        out_shape=(
            jax.ShapeDtypeStruct((rows, width), F32),
            jax.ShapeDtypeStruct((rows, width), BF16),
            jax.ShapeDtypeStruct((tokens, width), F32),
        ),
        in_specs=[vmem, vmem, smem, smem, vmem, vmem, vmem],
        out_specs=(vmem, vmem, vmem),
        scratch_shapes=[
            pltpu.VMEM((tokens, width), BF16),
            pltpu.VMEM((depth, width), BF16),
            pltpu.VMEM((nz, rows, width), BF16),
            pltpu.VMEM((nz - 1, rows, width), BF16),
            pltpu.VMEM((nz - 1, rows, width), BF16),
            pltpu.VMEM((SUB, width), F32),
            pltpu.VMEM((n_pol, rows, cw), BF16),
            pltpu.VMEM((n_pol - 1, rows, cw), BF16),
            pltpu.VMEM((rows, cw), F32),
            pltpu.VMEM((n_pol, depth, cw), BF16),
            pltpu.VMEM((8, width), F32),
            pltpu.VMEM((8, cw), F32),
            pltpu.VMEM((n_zero, 2, 8, 128), F32),
            pltpu.VMEM((n_pol, 2, 8, 128), F32),
            dma((nz,)), dma((nz,)),
            dma((nz - 1, CHUNKS)), dma((nz - 1, CHUNKS)),
            dma((nz - 1, CHUNKS)), dma((nz - 1, CHUNKS)),
            dma((n_pol - 1, CHUNKS)), dma((n_pol - 1, CHUNKS)),
            dma((n_zero,)), dma((n_zero,)),
            dma((n_pol,)), dma((n_pol,)),
            dma((lanes, n_zero)), dma((2, nz)), dma((lanes, nz)), dma((lanes, nz)), dma((2, nz)),
        ],
        compiler_params=pltpu.CompilerParams(
            collective_id=0, has_side_effects=True, vmem_limit_bytes=63 * 1024 * 1024
        ),
        cost_estimate=pl.CostEstimate(
            flops=4 * tokens * depth * width, bytes_accessed=24 * 1024 * 1024, transcendentals=0
        ),
    )(acts[0], cotan[0], advantage, merge_ratio, weight[0], anchor[0], init)
    return anchor_new[None], merged, result[None]


def solution(mesh):
    placed = (
        P("policy", "zero", None),
        P("policy", "zero", None),
        P("policy", "zero"),
        P(),
        P("policy", "zero", None),
        P("policy", "zero", None),
        P("zero", None),
    )
    return jax.shard_map(
        functools.partial(on_device, mesh.shape["policy"], mesh.shape["zero"]),
        mesh=mesh,
        in_specs=placed,
        out_specs=(P("policy", "zero", None), P("zero", None), P("policy", "zero", None)),
        check_vma=False,
    )
```

```python
import functools
import math

import jax
import jax.numpy as jnp
from jax import lax
from jax.experimental import pallas as pl
from jax.experimental.pallas import tpu as pltpu
from jax.sharding import PartitionSpec as P

SEQ = 128
STEP = 0.02
DECAY = 0.9
CHUNKS = 3
SUB = 16
F32 = jnp.float32
BF16 = jnp.bfloat16
MESH = pl.DeviceIdType.MESH


def flip(index, mask):
    out, bit = 0, 1
    while bit <= mask:
        digit = (index // bit) % 2
        out = out + bit * ((1 - digit) if mask & bit else digit)
        bit *= 2
    return out + (index // bit) * bit


def remote(src, dst, send, recv, **where):
    return pltpu.make_async_remote_copy(
        src_ref=src, dst_ref=dst, send_sem=send, recv_sem=recv, device_id=where, device_id_type=MESH
    )


def kernel(
    n_pol, n_zero, total_tokens,
    acts, cotan, adv, ratio, weight, anchor, init,
    anchor_out, merged_out, result,
    scaled, part, sib, up, dn, grad, ubuf, prec, mixed, mg, nsq, msq, ztile, ptile,
    sib_s, sib_r, up_s, up_r, dn_s, dn_r, pol_s, pol_r, zs_s, zs_r, ps_s, ps_r, ag_r, line_s, peer_s, core_s, relay_s,
):
    p = lax.axis_index("policy")
    b = lax.axis_index("zero")
    z, c = b // 2, b % 2
    nz = n_zero // 2
    rows, width = init.shape
    depth = acts.shape[1]
    pair = 2 * rows
    cw = width // n_pol
    R = rows // CHUNKS
    other = b + 1 - 2 * c
    sends = []

    def post(cond, make):
        @pl.when(cond)
        def _():
            make().start()
        sends.append((cond, make))

    barrier = pltpu.get_barrier_semaphore()
    for j in range(1, n_zero):
        pl.semaphore_signal(barrier, inc=1, device_id={"zero": lax.rem(b + j, n_zero)}, device_id_type=MESH)
    for j in range(1, n_pol):
        pl.semaphore_signal(barrier, inc=1, device_id={"policy": flip(p, j)}, device_id_type=MESH)

    for s in range(adv.shape[1]):
        level = adv[0, s].astype(F32) * 0.25

        @pl.loop(0, SEQ // SUB)
        def _(i):
            at = pl.ds(pl.multiple_of(s * SEQ + i * SUB, SUB), SUB)
            scaled[at, :] = (cotan[at, :].astype(F32) * level).astype(BF16)

    nsq[...] = jnp.zeros_like(nsq)
    msq[...] = jnp.zeros_like(msq)
    pl.semaphore_wait(barrier, n_zero - 1 + n_pol - 1)

    T = 384

    def tiles(first, count):
        @pl.loop(0, count)
        def _(j):
            at = pl.ds(pl.multiple_of(first + j * T, 128), T)
            part[at, :] = lax.dot_general(
                acts[:, at], scaled[...], (((0,), (0,)), ((), ())), preferred_element_type=F32
            ).astype(BF16)

    def to_sibling(d):
        def make():
            src = part.at[pl.ds(pl.multiple_of(d * pair + (1 - c) * rows, 16), rows), :]
            return remote(src, sib.at[d], sib_s.at[d], sib_r.at[d], zero=other)
        make().start()
        sends.append((None, make))

    def sib_wait(d):
        remote(sib.at[d], sib.at[d], sib_s.at[d], sib_r.at[d], zero=other).wait_recv()

    ends = jnp.logical_or(z == 0, z == nz - 1)

    def relay(i, k, who):
        for (d, here, end, recv, r_sem, s_sem, slot, step) in (
            (nz - 1 - i, z < nz - 1 - i, z == 0, up, up_r, up_s, nz - 2 - i, 2),
            (i, z > i, z == nz - 1, dn, dn_r, dn_s, i, -2),
        ):
            mine = pl.ds(k * R, R)

            def make(k, i_back=0, d=d, slot=slot, step=step, recv=recv, s_sem=s_sem, r_sem=r_sem):
                dd, at = (d + i_back, slot + i_back) if step > 0 else (d - i_back, slot - i_back)
                src = part.at[pl.ds(pl.multiple_of(dd * pair + c * rows + k * R, 16), R), :]
                return remote(
                    src, recv.at[at, pl.ds(k * R, R), :], s_sem.at[at, k], r_sem.at[at, k], zero=b + step
                )

            def add(with_recv):
                @pl.loop(0, R // SUB)
                def _(t):
                    own = pl.ds(pl.multiple_of(d * pair + c * rows + k * R + t * SUB, SUB), SUB)
                    at = pl.ds(pl.multiple_of(k * R + t * SUB, SUB), SUB)
                    acc = part[own, :].astype(F32) + sib[d, at, :].astype(F32)
                    if with_recv:
                        acc = acc + recv[slot, at, :].astype(F32)
                    part[own, :] = acc.astype(BF16)

            if who == "ends":
                @pl.when(jnp.logical_and(here, end))
                def _():
                    if k == 0:
                        sib_wait(d)
                    add(False)
                    if i > 0:
                        make(k, 1).wait_send()
                    make(k).start()
            else:
                @pl.when(jnp.logical_and(here, jnp.logical_not(end)))
                def _():
                    if k == 0:
                        sib_wait(d)
                    remote(
                        recv.at[slot, mine, :], recv.at[slot, mine, :], s_sem.at[slot, k], r_sem.at[slot, k], zero=b
                    ).wait_recv()
                    add(True)
                    make(k).start()
                sends.append((jnp.logical_and(here, jnp.logical_or(jnp.logical_not(end), i == nz - 2)),
                              functools.partial(make, k)))

    order = []
    for i in range((nz + 1) // 2):
        order += [nz - 1 - i] + ([i] if i != nz - 1 - i else [])
    upper = (2 * z) // nz
    order = [d + upper * (nz - 1 - 2 * d) for d in order]
    if pair % T == 0:
        for n, d in enumerate(order):
            tiles(d * pair, pair // T)
            to_sibling(d)
            if n == 1:
                relay(0, 0, "ends")
    else:
        tiles(0, depth // T)
        for d in order:
            to_sibling(d)
        relay(0, 0, "ends")

    share = jnp.full((8, 128), ratio[p].astype(F32), F32)
    whole = 0
    for q in range(n_pol):
        whole = whole + ratio[q]
    whole = jnp.full((8, 128), whole.astype(F32), F32)
    share = (share / whole)[0:1, 0:1]
    factor = STEP / math.sqrt(total_tokens)

    def final(k):
        mine = pl.ds(k * R, R)
        if k == 0:
            sib_wait(z)

        @pl.when(z > 0)
        def _():
            slot = z - 1
            remote(up.at[slot, mine, :], up.at[slot, mine, :], up_s.at[slot, k], up_r.at[slot, k], zero=b).wait_recv()

        @pl.when(z < nz - 1)
        def _():
            remote(dn.at[z, mine, :], dn.at[z, mine, :], dn_s.at[z, k], dn_r.at[z, k], zero=b).wait_recv()

        @pl.loop(0, R // SUB)
        def _(t):
            at = pl.ds(pl.multiple_of(k * R + t * SUB, SUB), SUB)
            own = pl.ds(pl.multiple_of(b * rows + k * R + t * SUB, SUB), SUB)
            grad[...] = part[own, :].astype(F32) + sib[z, at, :].astype(F32)

            @pl.when(z > 0)
            def _():
                grad[...] += up[z - 1, at, :].astype(F32)

            @pl.when(z < nz - 1)
            def _():
                grad[...] += dn[z, at, :].astype(F32)

            updated = weight[at, :].astype(F32) - factor * grad[...]
            anchor_out[at, :] = DECAY * anchor[at, :] + (1.0 - DECAY) * updated
            task = updated - init[at, :].astype(F32)
            sq = task * task
            nsq[...] += sq[:8] + sq[8:]
            term = (share * updated).astype(BF16)
            for q in range(n_pol):
                ubuf[q, at, :] = term[:, q * cw:(q + 1) * cw]

        for j in range(1, n_pol):
            to_policy(k, j).start()

    def to_policy(k, j):
        mine = pl.ds(k * R, R)
        return remote(
            ubuf.at[flip(p, j), mine, :], prec.at[j - 1, mine, :], pol_s.at[j - 1, k], pol_r.at[j - 1, k],
            policy=flip(p, j)
        )

    columns = pl.ds(pl.multiple_of(p * cw, 128), cw)

    def mix(k):
        mine = pl.ds(k * R, R)
        for j in range(1, n_pol):
            ref = prec.at[j - 1, mine, :]
            remote(ref, ref, pol_s.at[j - 1, k], pol_r.at[j - 1, k], policy=p).wait_recv()

        @pl.loop(0, R // SUB)
        def _(t):
            at = pl.ds(pl.multiple_of(k * R + t * SUB, SUB), SUB)
            acc = ubuf[p, at, :].astype(F32)
            for j in range(1, n_pol):
                acc = acc + prec[j - 1, at, :].astype(F32)
            acc = acc - init[at, columns].astype(F32)
            mixed[at, :] = acc
            sq = acc * acc
            msq[...] += sq[:8] + sq[8:]

    turn = jnp.where(ends, min(1, nz - 2), jnp.minimum(jnp.maximum(nz - 1 - z, z) + 1, nz - 2))
    for i in range(nz - 1):
        for k in range(CHUNKS):
            if i or k:
                relay(i, k, "ends")
            relay(i, k, "others")

            @pl.when(turn == i)
            def _():
                final(k)
                if k:
                    mix(k - 1)
                if k == CHUNKS - 1:
                    mix(k)
    for k in range(CHUNKS):
        for j in range(1, n_pol):
            sends.append((None, functools.partial(to_policy, k, j)))

    ztile[b, 0] = jnp.full((8, 128), jnp.sum(nsq[...]), F32)
    ztile[b, 1] = jnp.full((8, 128), jnp.sum(msq[...]), F32)
    for j in range(1, n_zero):
        def make(j=j):
            return remote(ztile.at[b], ztile.at[b], zs_s.at[j], zs_r.at[j], zero=lax.rem(b + j, n_zero))
        make().start()
        sends.append((None, make))
    result[...] = jnp.zeros_like(result)
    for j in range(1, n_zero):
        ref = ztile.at[lax.rem(b + n_zero - j, n_zero)]
        remote(ref, ref, zs_s.at[j], zs_r.at[j], zero=b).wait_recv()
    ptile[p, 0] = jnp.sum(ztile[:, 0], axis=0)
    ptile[p, 1] = jnp.sum(ztile[:, 1], axis=0)
    for j in range(1, n_pol):
        def make(j=j):
            return remote(ptile.at[p], ptile.at[p], ps_s.at[j], ps_r.at[j], policy=flip(p, j))
        make().start()
        sends.append((None, make))
    for j in range(1, n_pol):
        ref = ptile.at[flip(p, j)]
        remote(ref, ref, ps_s.at[j], ps_r.at[j], policy=p).wait_recv()
    target = jnp.zeros((8, 128), F32)
    mixed_sq = jnp.zeros((8, 128), F32)
    for q in range(n_pol):
        target = target + jnp.full((8, 128), ratio[q].astype(F32), F32) / whole * jnp.sqrt(ptile[q, 0])
        mixed_sq = mixed_sq + ptile[q, 1]
    scale = (target / jnp.sqrt(mixed_sq))[0:1, 0:1]

    @pl.loop(0, rows // SUB)
    def _(t):
        at = pl.ds(pl.multiple_of(t * SUB, SUB), SUB)
        own = pl.ds(pl.multiple_of(b * rows + t * SUB, SUB), SUB)
        mg[p, own, :] = (init[at, columns].astype(F32) + mixed[at, :] * scale).astype(BF16)

    square = n_pol == 4
    direct = (1, 2) if square else tuple(range(1, n_pol))
    half = rows // 2

    def piece(q, block):
        return mg.at[q, pl.ds(pl.multiple_of(block * rows, 16), rows), :]

    def halves(q, block, h):
        return mg.at[q, pl.ds(pl.multiple_of(block * rows + h * half, 16), half), :]

    def arrived(ref, sem):
        remote(ref, ref, sem, sem, zero=b).wait_recv()

    def offsets(t):
        if t < 0 or t >= nz:
            return []
        return [0] if t == 0 else [-t, t]

    def valid(o):
        return jnp.logical_and(z + o >= 0, z + o < nz)

    def stage_line(t):
        for o in offsets(t):
            ok = valid(o)
            zz = z + o
            bb = 2 * zz + c
            if t:
                @pl.when(ok)
                def _():
                    arrived(piece(p, bb), ag_r.at[0, bb])
            if o <= 0:
                post(jnp.logical_and(ok, z < nz - 1), lambda zz=zz, bb=bb: remote(
                    piece(p, bb), piece(p, bb), line_s.at[0, zz], ag_r.at[0, bb], zero=b + 2))
            if o >= 0:
                post(jnp.logical_and(ok, z > 0), lambda zz=zz, bb=bb: remote(
                    piece(p, bb), piece(p, bb), line_s.at[1, zz], ag_r.at[0, bb], zero=b - 2))
            for j in direct:
                post(ok, lambda zz=zz, bb=bb, j=j: remote(
                    piece(p, bb), piece(p, bb), peer_s.at[j, zz], ag_r.at[j, bb], policy=flip(p, j)))
            post(ok, lambda zz=zz, bb=bb: remote(
                piece(p, bb), piece(p, bb), core_s.at[0, zz], ag_r.at[0, bb], zero=other))

    def stage_peer(t):
        for o in offsets(t):
            ok = valid(o)
            zz = z + o
            bb = 2 * zz + c
            for j in direct:
                q = flip(p, j)

                @pl.when(ok)
                def _(j=j, q=q):
                    arrived(piece(q, bb), ag_r.at[j, bb])
                if square:
                    post(ok, lambda zz=zz, bb=bb, j=j, q=q: remote(
                        halves(q, bb, j - 1), halves(q, bb, j - 1), relay_s.at[j - 1, zz], ag_r.at[2 + j, bb],
                        policy=flip(p, 3 - j)))
                post(ok, lambda zz=zz, bb=bb, j=j, q=q: remote(
                    piece(q, bb), piece(q, bb), core_s.at[j, zz], ag_r.at[j, bb], zero=other))

    def stage_diagonal(t):
        if not square:
            return
        for o in offsets(t):
            ok = valid(o)
            zz = z + o
            bb = 2 * zz + c
            q = flip(p, 3)
            for h in (0, 1):
                @pl.when(ok)
                def _(h=h):
                    arrived(halves(q, bb, h), ag_r.at[3 + h, bb])
                post(ok, lambda zz=zz, bb=bb, h=h, q=q: remote(
                    halves(q, bb, h), halves(q, bb, h), core_s.at[3 + h, zz], ag_r.at[3 + h, bb], zero=other))

    def multiply(first, count):
        k_at = pl.ds(pl.multiple_of(first, 128), count)

        @pl.loop(0, n_pol)
        def _(q):
            n_at = pl.ds(pl.multiple_of(q * cw, 128), cw)
            result[:, n_at] += jnp.dot(acts[:, k_at], mg[q, k_at, :], preferred_element_type=F32)

    def stage_multiply(t):
        for o in offsets(t):
            zz = z + o
            bs = 2 * zz + 1 - c

            @pl.when(valid(o))
            def _():
                arrived(piece(p, bs), ag_r.at[0, bs])
                for j in direct:
                    arrived(piece(flip(p, j), bs), ag_r.at[j, bs])
                if square:
                    for h in (0, 1):
                        arrived(halves(flip(p, 3), bs, h), ag_r.at[3 + h, bs])
                if pair % 128 == 0:
                    multiply(zz * pair, pair)

    for t in range(nz + 3):
        stage_line(t)
        stage_peer(t - 1)
        stage_diagonal(t - 2)
        stage_multiply(t - 3)
    if pair % 128 != 0:
        tile = math.lcm(pair, 128)

        @pl.loop(0, depth // tile)
        def _(i):
            multiply(i * tile, tile)

    for q in range(n_pol):
        merged_out[:, q * cw:(q + 1) * cw] = mg[q, pl.ds(pl.multiple_of(b * rows, 16), rows), :]

    for cond, make in sends:
        if cond is None:
            make().wait_send()
        else:
            @pl.when(cond)
            def _(make=make):
                make().wait_send()


def on_device(n_pol, n_zero, acts, cotan, advantage, merge_ratio, weight, anchor, init):
    tokens, depth = acts.shape[1:]
    rows, width = init.shape
    nz, cw = n_zero // 2, width // n_pol
    dma = pltpu.SemaphoreType.DMA
    vmem = pl.BlockSpec(memory_space=pltpu.VMEM)
    smem = pl.BlockSpec(memory_space=pltpu.SMEM)
    lanes = max(n_pol, 5)
    anchor_new, merged, result = pl.pallas_call(
        functools.partial(kernel, n_pol, n_zero, tokens * n_zero),
        out_shape=(
            jax.ShapeDtypeStruct((rows, width), F32),
            jax.ShapeDtypeStruct((rows, width), BF16),
            jax.ShapeDtypeStruct((tokens, width), F32),
        ),
        in_specs=[vmem, vmem, smem, smem, vmem, vmem, vmem],
        out_specs=(vmem, vmem, vmem),
        scratch_shapes=[
            pltpu.VMEM((tokens, width), BF16),
            pltpu.VMEM((depth, width), BF16),
            pltpu.VMEM((nz, rows, width), BF16),
            pltpu.VMEM((nz - 1, rows, width), BF16),
            pltpu.VMEM((nz - 1, rows, width), BF16),
            pltpu.VMEM((SUB, width), F32),
            pltpu.VMEM((n_pol, rows, cw), BF16),
            pltpu.VMEM((n_pol - 1, rows, cw), BF16),
            pltpu.VMEM((rows, cw), F32),
            pltpu.VMEM((n_pol, depth, cw), BF16),
            pltpu.VMEM((8, width), F32),
            pltpu.VMEM((8, cw), F32),
            pltpu.VMEM((n_zero, 2, 8, 128), F32),
            pltpu.VMEM((n_pol, 2, 8, 128), F32),
            dma((nz,)), dma((nz,)),
            dma((nz - 1, CHUNKS)), dma((nz - 1, CHUNKS)),
            dma((nz - 1, CHUNKS)), dma((nz - 1, CHUNKS)),
            dma((n_pol - 1, CHUNKS)), dma((n_pol - 1, CHUNKS)),
            dma((n_zero,)), dma((n_zero,)),
            dma((n_pol,)), dma((n_pol,)),
            dma((lanes, n_zero)), dma((2, nz)), dma((lanes, nz)), dma((lanes, nz)), dma((2, nz)),
        ],
        compiler_params=pltpu.CompilerParams(
            collective_id=0, has_side_effects=True, vmem_limit_bytes=63 * 1024 * 1024
        ),
        cost_estimate=pl.CostEstimate(
            flops=4 * tokens * depth * width, bytes_accessed=24 * 1024 * 1024, transcendentals=0
        ),
    )(acts[0], cotan[0], advantage, merge_ratio, weight[0], anchor[0], init)
    return anchor_new[None], merged, result[None]


def solution(mesh):
    placed = (
        P("policy", "zero", None),
        P("policy", "zero", None),
        P("policy", "zero"),
        P(),
        P("policy", "zero", None),
        P("policy", "zero", None),
        P("zero", None),
    )
    return jax.shard_map(
        functools.partial(on_device, mesh.shape["policy"], mesh.shape["zero"]),
        mesh=mesh,
        in_specs=placed,
        out_specs=(P("policy", "zero", None), P("zero", None), P("policy", "zero", None)),
        check_vma=False,
    )
```

```python
import functools
import math

import jax
import jax.numpy as jnp
from jax import lax
from jax.experimental import pallas as pl
from jax.experimental.pallas import tpu as pltpu
from jax.sharding import PartitionSpec as P

SEQ = 128
STEP = 0.02
DECAY = 0.9
CHUNKS = 3
SUB = 16
F32 = jnp.float32
BF16 = jnp.bfloat16
MESH = pl.DeviceIdType.MESH


def flip(index, mask):
    out, bit = 0, 1
    while bit <= mask:
        digit = (index // bit) % 2
        out = out + bit * ((1 - digit) if mask & bit else digit)
        bit *= 2
    return out + (index // bit) * bit


def remote(src, dst, send, recv, **where):
    return pltpu.make_async_remote_copy(
        src_ref=src, dst_ref=dst, send_sem=send, recv_sem=recv, device_id=where, device_id_type=MESH
    )


def kernel(
    n_pol, n_zero, total_tokens,
    acts, cotan, adv, ratio, weight, anchor, init,
    anchor_out, merged_out, result,
    scaled, part, sib, up, dn, grad, ubuf, prec, base, mg, second, nsq, msq, ztile, ptile,
    sib_s, sib_r, up_s, up_r, dn_s, dn_r, pol_s, pol_r, zs_s, zs_r, ps_s, ps_r, ag_r, line_s, peer_s, core_s, relay_s, load_s,
):
    p = lax.axis_index("policy")
    b = lax.axis_index("zero")
    z, c = b // 2, b % 2
    nz = n_zero // 2
    rows, width = init.shape
    depth = acts.shape[1]
    pair = 2 * rows
    cw = width // n_pol
    R = rows // CHUNKS
    other = b + 1 - 2 * c
    sends = []

    def post(cond, make):
        @pl.when(cond)
        def _():
            make().start()
        sends.append((cond, make))

    barrier = pltpu.get_barrier_semaphore()
    for j in range(1, n_zero):
        pl.semaphore_signal(barrier, inc=1, device_id={"zero": lax.rem(b + j, n_zero)}, device_id_type=MESH)
    for j in range(1, n_pol):
        pl.semaphore_signal(barrier, inc=1, device_id={"policy": flip(p, j)}, device_id_type=MESH)

    load = pltpu.make_async_copy(cotan, scaled, load_s.at[0])
    load_anchor = pltpu.make_async_copy(anchor, anchor_out, load_s.at[1])
    load.start()
    load_anchor.start()
    load.wait()
    for s in range(adv.shape[1]):
        level = adv[0, s].astype(F32) * 0.25

        @pl.loop(0, SEQ // SUB)
        def _(i):
            at = pl.ds(pl.multiple_of(s * SEQ + i * SUB, SUB), SUB)
            scaled[at, :] = (scaled[at, :].astype(F32) * level).astype(BF16)

    nsq[...] = jnp.zeros_like(nsq)
    msq[...] = jnp.zeros_like(msq)
    result[...] = jnp.zeros_like(result)
    second[...] = jnp.zeros_like(second)
    square = n_pol == 4
    direct = (1, 2) if square else tuple(range(1, n_pol))
    half = rows // 2

    def piece(w, q, block):
        return (base, mg)[w].at[q, pl.ds(pl.multiple_of(block * rows, 16), rows), :]

    def halves(w, q, block, h):
        return (base, mg)[w].at[q, pl.ds(pl.multiple_of(block * rows + h * half, 16), half), :]

    def arrived(ref, sem):
        remote(ref, ref, sem, sem, zero=b).wait_recv()

    def offsets(t):
        if t < 0 or t >= nz:
            return []
        return [0] if t == 0 else [-t, t]

    def valid(o, kind):
        zz = z + o
        ok = jnp.logical_and(zz >= 0, zz < nz)
        outer = jnp.logical_or(zz == 0, zz == nz - 1)
        if kind == "outer":
            return jnp.logical_and(ok, outer)
        if kind == "inner":
            return jnp.logical_and(ok, jnp.logical_not(outer))
        return ok

    def stage_line(t, w, kind):
        for o in offsets(t):
            ok = valid(o, kind)
            zz = z + o
            bb = 2 * zz + c
            if t:
                @pl.when(ok)
                def _():
                    arrived(piece(w, p, bb), ag_r.at[w, 0, bb])
            if o <= 0:
                post(jnp.logical_and(ok, z < nz - 1), lambda zz=zz, bb=bb: remote(
                    piece(w, p, bb), piece(w, p, bb), line_s.at[w, 0, zz], ag_r.at[w, 0, bb], zero=b + 2))
            if o >= 0:
                post(jnp.logical_and(ok, z > 0), lambda zz=zz, bb=bb: remote(
                    piece(w, p, bb), piece(w, p, bb), line_s.at[w, 1, zz], ag_r.at[w, 0, bb], zero=b - 2))
            for j in direct:
                post(ok, lambda zz=zz, bb=bb, j=j: remote(
                    piece(w, p, bb), piece(w, p, bb), peer_s.at[w, j, zz], ag_r.at[w, j, bb], policy=flip(p, j)))
            post(ok, lambda zz=zz, bb=bb: remote(
                piece(w, p, bb), piece(w, p, bb), core_s.at[w, 0, zz], ag_r.at[w, 0, bb], zero=other))

    def stage_peer(t, w, kind):
        for o in offsets(t):
            ok = valid(o, kind)
            zz = z + o
            bb = 2 * zz + c
            for j in direct:
                q = flip(p, j)

                @pl.when(ok)
                def _(j=j, q=q):
                    arrived(piece(w, q, bb), ag_r.at[w, j, bb])
                if square:
                    post(ok, lambda zz=zz, bb=bb, j=j, q=q: remote(
                        halves(w, q, bb, j - 1), halves(w, q, bb, j - 1), relay_s.at[w, j - 1, zz], ag_r.at[w, 2 + j, bb],
                        policy=flip(p, 3 - j)))
                post(ok, lambda zz=zz, bb=bb, j=j, q=q: remote(
                    piece(w, q, bb), piece(w, q, bb), core_s.at[w, j, zz], ag_r.at[w, j, bb], zero=other))

    def stage_diagonal(t, w, kind):
        if not square:
            return
        for o in offsets(t):
            ok = valid(o, kind)
            zz = z + o
            bb = 2 * zz + c
            q = flip(p, 3)
            for h in (0, 1):
                @pl.when(ok)
                def _(h=h):
                    arrived(halves(w, q, bb, h), ag_r.at[w, 3 + h, bb])
                post(ok, lambda zz=zz, bb=bb, h=h, q=q: remote(
                    halves(w, q, bb, h), halves(w, q, bb, h), core_s.at[w, 3 + h, zz], ag_r.at[w, 3 + h, bb], zero=other))

    def multiply(w, first, count):
        k_at = pl.ds(pl.multiple_of(first, 128), count)
        src, out = (base, mg)[w], (result, second)[w]

        @pl.loop(0, n_pol)
        def _(q):
            n_at = pl.ds(pl.multiple_of(q * cw, 128), cw)
            out[:, n_at] += jnp.dot(acts[:, k_at], src[q, k_at, :], preferred_element_type=F32)

    def stage_multiply(t, w, kind):
        for o in offsets(t):
            zz = z + o
            bs = 2 * zz + 1 - c

            @pl.when(valid(o, kind))
            def _():
                arrived(piece(w, p, bs), ag_r.at[w, 0, bs])
                for j in direct:
                    arrived(piece(w, flip(p, j), bs), ag_r.at[w, j, bs])
                if square:
                    for h in (0, 1):
                        arrived(halves(w, flip(p, 3), bs, h), ag_r.at[w, 3 + h, bs])

        if pair % 128 == 0 and offsets(t):
            @pl.loop(0, 1 + (t > 0))
            def _(i):
                o = 2 * t * i - t

                @pl.when(valid(o, kind))
                def _():
                    multiply(w, (z + o) * pair, pair)

    def gather(t, w, kind):
        stage_line(t, w, kind)
        stage_peer(t - 1, w, kind)
        stage_diagonal(t - 2, w, kind)
        stage_multiply(t - 3, w, kind)

    last = nz + 2
    columns = pl.ds(pl.multiple_of(p * cw, 128), cw)

    @pl.loop(0, rows // SUB)
    def _(t):
        at = pl.ds(pl.multiple_of(t * SUB, SUB), SUB)
        own = pl.ds(pl.multiple_of(b * rows + t * SUB, SUB), SUB)
        base[p, own, :] = init[at, columns]

    pl.semaphore_wait(barrier, n_zero - 1 + n_pol - 1)
    gather(0, 0, None)

    T = 384

    def tiles(first, count):
        @pl.loop(0, count)
        def _(j):
            at = pl.ds(pl.multiple_of(first + j * T, 128), T)
            part[at, :] = lax.dot_general(
                acts[:, at], scaled[...], (((0,), (0,)), ((), ())), preferred_element_type=F32
            ).astype(BF16)

    def to_sibling(d):
        def make():
            src = part.at[pl.ds(pl.multiple_of(d * pair + (1 - c) * rows, 16), rows), :]
            return remote(src, sib.at[d], sib_s.at[d], sib_r.at[d], zero=other)
        make().start()
        sends.append((None, make))

    def sib_wait(d):
        remote(sib.at[d], sib.at[d], sib_s.at[d], sib_r.at[d], zero=other).wait_recv()

    ends = jnp.logical_or(z == 0, z == nz - 1)

    def relay(i, k, who):
        for (d, here, end, recv, r_sem, s_sem, slot, step) in (
            (nz - 1 - i, z < nz - 1 - i, z == 0, up, up_r, up_s, nz - 2 - i, 2),
            (i, z > i, z == nz - 1, dn, dn_r, dn_s, i, -2),
        ):
            mine = pl.ds(k * R, R)

            def make(k, i_back=0, d=d, slot=slot, step=step, recv=recv, s_sem=s_sem, r_sem=r_sem):
                dd, at = (d + i_back, slot + i_back) if step > 0 else (d - i_back, slot - i_back)
                src = part.at[pl.ds(pl.multiple_of(dd * pair + c * rows + k * R, 16), R), :]
                return remote(
                    src, recv.at[at, pl.ds(k * R, R), :], s_sem.at[at, k], r_sem.at[at, k], zero=b + step
                )

            def add(with_recv):
                @pl.loop(0, R // SUB)
                def _(t):
                    own = pl.ds(pl.multiple_of(d * pair + c * rows + k * R + t * SUB, SUB), SUB)
                    at = pl.ds(pl.multiple_of(k * R + t * SUB, SUB), SUB)
                    acc = part[own, :].astype(F32) + sib[d, at, :].astype(F32)
                    if with_recv:
                        acc = acc + recv[slot, at, :].astype(F32)
                    part[own, :] = acc.astype(BF16)

            if who == "ends":
                @pl.when(jnp.logical_and(here, end))
                def _():
                    if k == 0:
                        sib_wait(d)
                    add(False)
                    if i > 0:
                        make(k, 1).wait_send()
                    make(k).start()
            else:
                @pl.when(jnp.logical_and(here, jnp.logical_not(end)))
                def _():
                    if k == 0:
                        sib_wait(d)
                    remote(
                        recv.at[slot, mine, :], recv.at[slot, mine, :], s_sem.at[slot, k], r_sem.at[slot, k], zero=b
                    ).wait_recv()
                    add(True)
                    make(k).start()
                sends.append((jnp.logical_and(here, jnp.logical_or(jnp.logical_not(end), i == nz - 2)),
                              functools.partial(make, k)))

    order = []
    for i in range((nz + 1) // 2):
        order += [nz - 1 - i] + ([i] if i != nz - 1 - i else [])
    upper = (2 * z) // nz
    order = [d + upper * (nz - 1 - 2 * d) for d in order]
    if pair % T == 0:
        for n, d in enumerate(order):
            tiles(d * pair, pair // T)
            to_sibling(d)
            if n == 1:
                relay(0, 0, "ends")
    else:
        tiles(0, depth // T)
        for d in order:
            to_sibling(d)
        relay(0, 0, "ends")

    load_anchor.wait()
    share = jnp.full((8, 128), ratio[p].astype(F32), F32)
    whole = 0
    for q in range(n_pol):
        whole = whole + ratio[q]
    whole = jnp.full((8, 128), whole.astype(F32), F32)
    share = (share / whole)[0:1, 0:1]
    factor = STEP / math.sqrt(total_tokens)

    def final(k):
        mine = pl.ds(k * R, R)
        if k == 0:
            sib_wait(z)

        @pl.when(z > 0)
        def _():
            slot = z - 1
            remote(up.at[slot, mine, :], up.at[slot, mine, :], up_s.at[slot, k], up_r.at[slot, k], zero=b).wait_recv()

        @pl.when(z < nz - 1)
        def _():
            remote(dn.at[z, mine, :], dn.at[z, mine, :], dn_s.at[z, k], dn_r.at[z, k], zero=b).wait_recv()

        @pl.loop(0, R // SUB)
        def _(t):
            at = pl.ds(pl.multiple_of(k * R + t * SUB, SUB), SUB)
            own = pl.ds(pl.multiple_of(b * rows + k * R + t * SUB, SUB), SUB)
            grad[...] = part[own, :].astype(F32) + sib[z, at, :].astype(F32)

            @pl.when(z > 0)
            def _():
                grad[...] += up[z - 1, at, :].astype(F32)

            @pl.when(z < nz - 1)
            def _():
                grad[...] += dn[z, at, :].astype(F32)

            updated = weight[at, :].astype(F32) - factor * grad[...]
            anchor_out[at, :] = DECAY * anchor_out[at, :] + (1.0 - DECAY) * updated
            task = updated - init[at, :].astype(F32)
            sq = task * task
            nsq[...] += sq[:8] + sq[8:]
            term = (share * updated).astype(BF16)
            for q in range(n_pol):
                ubuf[q, at, :] = term[:, q * cw:(q + 1) * cw]

        for j in range(1, n_pol):
            to_policy(k, j).start()

    def to_policy(k, j):
        mine = pl.ds(k * R, R)
        return remote(
            ubuf.at[flip(p, j), mine, :], prec.at[j - 1, mine, :], pol_s.at[j - 1, k], pol_r.at[j - 1, k],
            policy=flip(p, j)
        )

    columns = pl.ds(pl.multiple_of(p * cw, 128), cw)

    def mix(k):
        mine = pl.ds(k * R, R)
        for j in range(1, n_pol):
            ref = prec.at[j - 1, mine, :]
            remote(ref, ref, pol_s.at[j - 1, k], pol_r.at[j - 1, k], policy=p).wait_recv()

        @pl.loop(0, R // SUB)
        def _(t):
            at = pl.ds(pl.multiple_of(k * R + t * SUB, SUB), SUB)
            acc = ubuf[p, at, :].astype(F32)
            for j in range(1, n_pol):
                acc = acc + prec[j - 1, at, :].astype(F32)
            mg[p, pl.ds(pl.multiple_of(b * rows + k * R + t * SUB, SUB), SUB), :] = acc.astype(BF16)
            acc = acc - init[at, columns].astype(F32)
            sq = acc * acc
            msq[...] += sq[:8] + sq[8:]

    turn = jnp.where(ends, min(1, nz - 2), jnp.minimum(jnp.maximum(nz - 1 - z, z) + 1, nz - 2))
    for i in range(nz - 1):
        for k in range(CHUNKS):
            if i or k:
                relay(i, k, "ends")
            relay(i, k, "others")

            @pl.when(turn == i)
            def _():
                final(k)
                if k:
                    mix(k - 1)
                if k == CHUNKS - 1:
                    mix(k)

            n = i * CHUNKS + k
            if 1 <= n + 1 <= last:
                gather(n + 1, 0, None)
            m = n - (min(1, nz - 2) * CHUNKS + CHUNKS - 1)
            if 0 <= m <= last:
                gather(m, 1, "outer")
    for k in range(CHUNKS):
        for j in range(1, n_pol):
            sends.append((None, functools.partial(to_policy, k, j)))

    done = n
    gather(0, 1, "inner")

    ztile[b, 0] = jnp.full((8, 128), jnp.sum(nsq[...]), F32)
    ztile[b, 1] = jnp.full((8, 128), jnp.sum(msq[...]), F32)
    for j in range(1, n_zero):
        def make(j=j):
            return remote(ztile.at[b], ztile.at[b], zs_s.at[j], zs_r.at[j], zero=lax.rem(b + j, n_zero))
        make().start()
        sends.append((None, make))
    for n in range(done + 2, last + 1):
        gather(n, 0, None)
    gather(m + 1, 1, "outer")
    gather(1, 1, "inner")
    for j in range(1, n_zero):
        ref = ztile.at[lax.rem(b + n_zero - j, n_zero)]
        remote(ref, ref, zs_s.at[j], zs_r.at[j], zero=b).wait_recv()
    ptile[p, 0] = jnp.sum(ztile[:, 0], axis=0)
    ptile[p, 1] = jnp.sum(ztile[:, 1], axis=0)
    for j in range(1, n_pol):
        def make(j=j):
            return remote(ptile.at[p], ptile.at[p], ps_s.at[j], ps_r.at[j], policy=flip(p, j))
        make().start()
        sends.append((None, make))
    for j in range(1, n_pol):
        ref = ptile.at[flip(p, j)]
        remote(ref, ref, ps_s.at[j], ps_r.at[j], policy=p).wait_recv()
    target = jnp.zeros((8, 128), F32)
    mixed_sq = jnp.zeros((8, 128), F32)
    for q in range(n_pol):
        target = target + jnp.full((8, 128), ratio[q].astype(F32), F32) / whole * jnp.sqrt(ptile[q, 0])
        mixed_sq = mixed_sq + ptile[q, 1]
    scale = (target / jnp.sqrt(mixed_sq))[0:1, 0:1]

    for n in range(2, last + 1):
        gather(n, 1, "inner")
        if m + n <= last:
            gather(m + n, 1, "outer")
    if pair % 128 != 0:
        tile = math.lcm(pair, 128)
        for w in (0, 1):
            @pl.loop(0, depth // tile)
            def _(i):
                multiply(w, i * tile, tile)

    @pl.loop(0, result.shape[0] // SUB)
    def _(t):
        at = pl.ds(pl.multiple_of(t * SUB, SUB), SUB)
        result[at, :] = (1.0 - scale) * result[at, :] + scale * second[at, :]

    @pl.loop(0, rows // SUB)
    def _(t):
        at = pl.ds(pl.multiple_of(t * SUB, SUB), SUB)
        own = pl.ds(pl.multiple_of(b * rows + t * SUB, SUB), SUB)
        for q in range(n_pol):
            start = init[at, q * cw:(q + 1) * cw].astype(F32)
            merged_out[at, q * cw:(q + 1) * cw] = (
                start + (mg[q, own, :].astype(F32) - start) * scale
            ).astype(BF16)

    for cond, make in sends:
        if cond is None:
            make().wait_send()
        else:
            @pl.when(cond)
            def _(make=make):
                make().wait_send()


def on_device(n_pol, n_zero, acts, cotan, advantage, merge_ratio, weight, anchor, init):
    tokens, depth = acts.shape[1:]
    rows, width = init.shape
    nz, cw = n_zero // 2, width // n_pol
    dma = pltpu.SemaphoreType.DMA
    vmem = pl.BlockSpec(memory_space=pltpu.VMEM)
    anywhere = pl.BlockSpec(memory_space=pl.ANY)
    smem = pl.BlockSpec(memory_space=pltpu.SMEM)
    lanes = max(n_pol, 5)
    anchor_new, merged, result = pl.pallas_call(
        functools.partial(kernel, n_pol, n_zero, tokens * n_zero),
        out_shape=(
            jax.ShapeDtypeStruct((rows, width), F32),
            jax.ShapeDtypeStruct((rows, width), BF16),
            jax.ShapeDtypeStruct((tokens, width), F32),
        ),
        in_specs=[vmem, anywhere, smem, smem, vmem, anywhere, vmem],
        out_specs=(vmem, vmem, vmem),
        scratch_shapes=[
            pltpu.VMEM((tokens, width), BF16),
            pltpu.VMEM((depth, width), BF16),
            pltpu.VMEM((nz, rows, width), BF16),
            pltpu.VMEM((nz - 1, rows, width), BF16),
            pltpu.VMEM((nz - 1, rows, width), BF16),
            pltpu.VMEM((SUB, width), F32),
            pltpu.VMEM((n_pol, rows, cw), BF16),
            pltpu.VMEM((n_pol - 1, rows, cw), BF16),
            pltpu.VMEM((n_pol, depth, cw), BF16),
            pltpu.VMEM((n_pol, depth, cw), BF16),
            pltpu.VMEM((tokens, width), F32),
            pltpu.VMEM((8, width), F32),
            pltpu.VMEM((8, cw), F32),
            pltpu.VMEM((n_zero, 2, 8, 128), F32),
            pltpu.VMEM((n_pol, 2, 8, 128), F32),
            dma((nz,)), dma((nz,)),
            dma((nz - 1, CHUNKS)), dma((nz - 1, CHUNKS)),
            dma((nz - 1, CHUNKS)), dma((nz - 1, CHUNKS)),
            dma((n_pol - 1, CHUNKS)), dma((n_pol - 1, CHUNKS)),
            dma((n_zero,)), dma((n_zero,)),
            dma((n_pol,)), dma((n_pol,)),
            dma((2, lanes, n_zero)), dma((2, 2, nz)), dma((2, lanes, nz)), dma((2, lanes, nz)), dma((2, 2, nz)), dma((2,)),
        ],
        compiler_params=pltpu.CompilerParams(
            collective_id=0, has_side_effects=True, vmem_limit_bytes=63 * 1024 * 1024
        ),
        cost_estimate=pl.CostEstimate(
            flops=4 * tokens * depth * width, bytes_accessed=24 * 1024 * 1024, transcendentals=0
        ),
    )(acts[0], cotan[0], advantage, merge_ratio, weight[0], anchor[0], init)
    return anchor_new[None], merged, result[None]


def solution(mesh):
    placed = (
        P("policy", "zero", None),
        P("policy", "zero", None),
        P("policy", "zero"),
        P(),
        P("policy", "zero", None),
        P("policy", "zero", None),
        P("zero", None),
    )
    return jax.shard_map(
        functools.partial(on_device, mesh.shape["policy"], mesh.shape["zero"]),
        mesh=mesh,
        in_specs=placed,
        out_specs=(P("policy", "zero", None), P("zero", None), P("policy", "zero", None)),
        check_vma=False,
    )
```
